512 devices in a mesh: dp: 64 (over y, x, core), tensor: 8 (over z).
Axes of the slice: x: 4, y: 8, z: 8, core: 2. Of those that a mesh axis runs over, the one named last changes fastest.
Arguments:
- queries: bfloat16 [98304, 4096], P('dp', 'tensor'), may hold values from -150 to 150
- key_rows: bfloat16 [98304, 1024], P('dp', 'tensor'), may hold values from -150 to 150
- values: bfloat16 [98304, 1024], P('dp', 'tensor'), may hold values from -6 to 6
- doc_lengths: int32 [64, 12], replicated, may hold values from 0 to 512, as said below
- swap_plan: int32 [64, 4], replicated, may hold values from -1 to 2, as said below
Outputs:
- attention_out: bfloat16 [98304, 4096], P(('dp', 'tensor'))
The draws below stay inside these ranges and needn't reach their ends.
Inputs may be any that keep to these rules, and one draw needn't show every extreme that they name: `doc_lengths`: each row lists its documents in order, each a multiple of 128 tokens; no document crosses a multiple of 512 tokens; the documents fill whole blocks from the row's start, zeros follow the last one, and every row has at least one block of documents. `swap_plan`: entry [r, s] names a block of row r; the row whose index differs from r in bit log2(64) - 1 - s has -1 at section s exactly when r has.
All inputs are finite; a program needn't handle non-finite values.
Results may differ from the reference program's by a relative error of at most 0.0045.
Values may be sent and summed in bfloat16 or wider, within the bound.
A program may use at most 64 MiB of HBM per device.

```python
import math
import jax
import jax.numpy as jnp
from jax import lax

HEADS = 32
KV_HEADS = 8
HEAD_DIM = 128
TILE = 128
BLOCK_TILES = 4
BLOCKS_DEV = 3
SECTIONS = 4
BLOCK = 512
ROW = 1536
DOCS = 12
TOKENS = 98304
N_DP = 64


def block_layout(key):
    rank_ids = jnp.arange(N_DP, dtype=jnp.int32)
    level_draw = jax.random.randint(jax.random.fold_in(key, 11), (N_DP,), 0, BLOCKS_DEV + 1)
    counts = jnp.clip(level_draw, 1, BLOCKS_DEV)
    half_ranks = N_DP // 2
    counts = jnp.where(rank_ids == 1, 1, counts)
    counts = jnp.where(rank_ids == 2, BLOCKS_DEV, counts)
    counts = jnp.where(rank_ids == 2 + half_ranks, 1, counts)
    counts = jnp.where(rank_ids == 0, 1, counts)
    counts = jnp.where(rank_ids == half_ranks, BLOCKS_DEV, counts)
    counts = jnp.where(rank_ids == N_DP - 1, 1, counts)
    counts = jnp.where(rank_ids == half_ranks - 1, BLOCKS_DEV, counts)
    tile_ids = jnp.arange(DOCS, dtype=jnp.int32)
    tile_block = tile_ids // BLOCK_TILES
    coin_flip = jax.random.randint(jax.random.fold_in(key, 12), (N_DP, DOCS), 0, 2)
    first_tile = (tile_ids % BLOCK_TILES == 0)[None, :]
    inner_start = (coin_flip == 1) & jnp.logical_not((rank_ids[:, None] == 0) & (tile_block[None, :] == 0))
    live_tiles = tile_block[None, :] < counts[:, None]
    doc_starts = ((first_tile | inner_start) & live_tiles).astype(jnp.int32)
    doc_index = jnp.cumsum(doc_starts, axis=1) - 1
    doc_slots = jnp.arange(DOCS, dtype=jnp.int32)
    membership = (doc_index[:, :, None] == doc_slots[None, None, :]) & live_tiles[:, :, None]
    lengths = TILE * jnp.sum(membership.astype(jnp.int32), axis=1)
    positions = jnp.arange(BLOCKS_DEV, dtype=jnp.int32)[None, :]
    live_blocks = (positions < counts[:, None]).astype(jnp.int32)
    levels = N_DP.bit_length() - 1
    columns = []
    for section_index in range(SECTIONS):
        partner = jnp.bitwise_xor(rank_ids, 1 << levels - 1 - section_index)
        filled = jnp.sum(live_blocks, axis=1)
        partner_fill = filled[partner]
        last_live = jnp.max(jnp.where(live_blocks == 1, positions, -1), axis=1)
        first_empty = jnp.min(jnp.where(live_blocks == 1, BLOCKS_DEV, positions), axis=1)
        chosen = jnp.where(filled - partner_fill >= 2, last_live, jnp.where(partner_fill - filled >= 2, first_empty, -1))
        safe_index = jnp.maximum(chosen, 0)
        incoming = live_blocks[partner, safe_index[partner]]
        current = live_blocks[rank_ids, safe_index]
        live_blocks = live_blocks.at[rank_ids, safe_index].set(jnp.where(chosen >= 0, incoming, current))
        columns.append(chosen)
    plan_table = jnp.stack(columns, axis=1)
    return (lengths.astype(jnp.int32), plan_table.astype(jnp.int32))


def draw_doc_lengths(key, part):
    lengths, plan_table = block_layout(key)
    return lengths


def draw_swap_plan(key, part):
    lengths, plan_table = block_layout(key)
    return plan_table


def draw_queries(key, part):
    own_key = jax.random.fold_in(key, 1)
    return jax.random.normal(own_key, (TOKENS, HEADS * HEAD_DIM), jnp.float32).astype(jnp.bfloat16)


def draw_key_rows(key, part):
    own_key = jax.random.fold_in(key, 2)
    return jax.random.normal(own_key, (TOKENS, KV_HEADS * HEAD_DIM), jnp.float32).astype(jnp.bfloat16)


def shard_levels(rng, extent, split, low, top_value):
    def one(axis_at, shards_of):
        steps = jax.random.uniform(jax.random.fold_in(jax.random.fold_in(rng, 6), axis_at), (shards_of,), jnp.float32, low / len(split), top_value / len(split))
        return jnp.repeat(jnp.exp(steps), extent[axis_at] // shards_of).reshape((-1,) + (1,) * (len(extent) - axis_at - 1))

    level = one(*split[0])
    for cut in split[1:]:
        level = level * one(*cut)
    return level


def normal_values(rng, shape, width, limit, pieces=(), kind=jnp.bfloat16):
    entries = width * jax.random.normal(rng, shape, jnp.float32)
    if pieces:
        entries = entries * shard_levels(rng, shape, pieces, -0.22, 0.18)
    return jnp.clip(entries, -limit, limit).astype(kind)


def setup_inputs(seed: int = 0) -> dict:
    keys = jax.random.split(jax.random.key(seed), 6)
    return {
        "queries": draw_queries(jax.random.fold_in(keys[5], 71), 0),
        "key_rows": draw_key_rows(jax.random.fold_in(keys[5], 71), 0),
        "values": normal_values(keys[2], (TOKENS, KV_HEADS * HEAD_DIM), 1.0, 6.0, ((0, 64), (1, 8))),
        "doc_lengths": draw_doc_lengths(jax.random.fold_in(keys[5], 71), 0),
        "swap_plan": draw_swap_plan(jax.random.fold_in(keys[5], 71), 0),
    }


def token_ids(lengths_row):
    endings = jnp.cumsum(lengths_row).astype(jnp.int32)
    places = jnp.arange(ROW, dtype=jnp.int32)
    counted = lax.optimization_barrier(jnp.sum((endings[None, :] <= places[:, None]).astype(jnp.int32), axis=1)).astype(jnp.int32)
    return jnp.where(places < endings[-1], counted, -1).astype(jnp.int32)

def attend_block(query_block, key_block, value_block, block_ids):
    group_size = HEADS // KV_HEADS
    query_four = query_block.astype(jnp.float32).reshape(BLOCK, KV_HEADS, group_size, HEAD_DIM)
    key_three = key_block.astype(jnp.float32).reshape(BLOCK, KV_HEADS, HEAD_DIM)
    value_three = value_block.astype(jnp.float32).reshape(BLOCK, KV_HEADS, HEAD_DIM)
    scores = jnp.einsum('qhgd,khd->hgqk', query_four, key_three) * (1.0 / math.sqrt(HEAD_DIM))
    places = jnp.arange(BLOCK, dtype=jnp.int32)
    allowed = (block_ids[:, None] == block_ids[None, :]) & (block_ids[:, None] >= 0) & (places[None, :] <= places[:, None])
    masked = jnp.where(allowed, scores, -1e+30)
    highest = lax.optimization_barrier(jnp.max(masked, axis=-1, keepdims=True))
    powers = jnp.where(allowed, jnp.exp(masked - highest), 0.0)
    totals = lax.optimization_barrier(jnp.sum(powers, axis=-1, keepdims=True))
    live_rows = block_ids >= 0
    weights = (powers / jnp.where(live_rows[:, None], totals, 1.0)).astype(jnp.bfloat16)
    head_mix = jnp.einsum('hgqk,khd->qhgd', weights.astype(jnp.float32), value_three)
    return head_mix.reshape(BLOCK, HEADS * HEAD_DIM).astype(jnp.bfloat16)

def flatten_rows(array):
    return array.reshape((N_DP * BLOCKS_DEV,) + array.shape[2:])

def attend_packed(packed):
    return attend_block(packed[0], packed[1], packed[2], packed[3])

def reference(queries, key_rows, values, doc_lengths, swap_plan):
    feature = HEADS * HEAD_DIM
    query_blocks = queries.reshape(N_DP, BLOCKS_DEV, BLOCK, feature)
    key_blocks = key_rows.reshape(N_DP, BLOCKS_DEV, BLOCK, KV_HEADS * HEAD_DIM)
    value_blocks = values.reshape(N_DP, BLOCKS_DEV, BLOCK, KV_HEADS * HEAD_DIM)
    id_blocks = jax.vmap(token_ids)(doc_lengths).reshape(N_DP, BLOCKS_DEV, BLOCK)
    attended = lax.map(attend_packed, (flatten_rows(query_blocks), flatten_rows(key_blocks), flatten_rows(value_blocks), flatten_rows(id_blocks)))
    attended = attended.reshape(N_DP, BLOCKS_DEV, BLOCK, feature)
    rank_ids = jnp.arange(N_DP, dtype=jnp.int32)
    levels = N_DP.bit_length() - 1
    for section_index in range(SECTIONS):
        partner = jnp.bitwise_xor(rank_ids, 1 << levels - 1 - section_index).astype(jnp.int32)
        chosen = swap_plan[:, section_index].astype(jnp.int32)
        safe_index = jnp.maximum(chosen, 0).astype(jnp.int32)
        incoming = attended[partner, safe_index[partner]]
        current = attended[rank_ids, safe_index]
        attended = attended.at[rank_ids, safe_index].set(jnp.where((chosen >= 0)[:, None, None], incoming, current))
    return attended.reshape(N_DP * ROW, feature)
```

```python
import math

import jax
import jax.numpy as jnp
from jax import lax
from jax.experimental import pallas as pl
from jax.experimental.pallas import tpu as pltpu
from jax.sharding import PartitionSpec as P

HEAD_DIM = 128
SECTIONS = 4
BLOCK = 512
TILE = 128
TILES = BLOCK // TILE
BLOCKS = 3
SUBS = 2
GRAIN = 64 // SUBS
GRAINS = BLOCK // GRAIN // SUBS
SCALE = math.log2(math.e) / math.sqrt(HEAD_DIM)
MESH = pl.DeviceIdType.MESH


def kernel(
    heads, shards, levels,
    q_ref, k_ref, v_ref, len_ref, plan_ref, out_ref,
    held, snd, rcv, fin, ids, s_sem, r_sem, as_sem, ar_sem, o_sem,
):
    row = lax.axis_index("dp")
    own = lax.axis_index("tensor")
    chunks = heads * SUBS
    share = BLOCKS * GRAINS // shards

    partners = []
    for section in range(SECTIONS):
        mask = 2 ** (levels - 1 - section)
        partners.append(row + mask * (1 - 2 * ((row // mask) % 2)))
    others = [(own + step) % shards for step in range(1, shards)]

    barrier = pltpu.get_barrier_semaphore()
    for partner in partners:
        pl.semaphore_signal(barrier, inc=1, device_id=(partner, own), device_id_type=MESH)
    for other in others:
        pl.semaphore_signal(barrier, inc=1, device_id=(row, other), device_id_type=MESH)

    endings = []
    total = jnp.int32(0)
    for doc in range(len_ref.shape[0]):
        total = total + len_ref[doc, row]
        endings.append(total)
    for tile in range(BLOCKS * TILES):
        count = jnp.int32(0)
        for ending in endings:
            count = count + jnp.where(ending <= tile * TILE, 1, 0)
        ids[tile] = jnp.where(tile * TILE < total, count, -1)

    lower = lax.broadcasted_iota(jnp.int32, (TILE, TILE), 0) >= lax.broadcasted_iota(
        jnp.int32, (TILE, TILE), 1
    )

    def attend(head):
        columns = slice(head * HEAD_DIM, (head + 1) * HEAD_DIM)

        def block(b, carry):
            start = pl.multiple_of(b * BLOCK, BLOCK)
            for i in range(TILES):
                keys = k_ref[pl.ds(start, (i + 1) * TILE), :]
                scores = lax.dot_general(
                    q_ref[pl.ds(start + i * TILE, TILE), columns], keys,
                    (((1,), (1,)), ((), ())), preferred_element_type=jnp.float32,
                )
                doc = ids[b * TILES + i]
                parts = [
                    scores[:, j * TILE : (j + 1) * TILE]
                    + jnp.where(ids[b * TILES + j] == doc, 0.0, -1e30)
                    for j in range(i)
                ]
                parts.append(jnp.where(lower, scores[:, i * TILE :], -1e30))
                masked = jnp.concatenate(parts, axis=1) if i else parts[0]
                highest = jnp.max(masked, axis=1, keepdims=True)
                powers = jnp.exp2((masked - highest) * SCALE)
                live = jnp.where(doc >= 0, 1.0, 0.0)
                weights = powers * (live / jnp.sum(powers, axis=1, keepdims=True))
                mixed = jnp.dot(
                    weights.astype(jnp.bfloat16), v_ref[pl.ds(start, (i + 1) * TILE), :],
                    preferred_element_type=jnp.float32,
                ).astype(jnp.bfloat16)
                for g in range(TILE // GRAIN):
                    at = i * (TILE // GRAIN) + g
                    held[head * SUBS + at % SUBS, b * GRAINS + at // SUBS] = mixed[
                        g * GRAIN : (g + 1) * GRAIN
                    ]
            return carry

        lax.fori_loop(0, BLOCKS, block, 0)

    def swap_copy(section, c):
        return pltpu.make_async_remote_copy(
            src_ref=snd.at[section, c], dst_ref=rcv.at[section, c],
            send_sem=s_sem.at[section, c], recv_sem=r_sem.at[section, c],
            device_id=(partners[section], own), device_id_type=MESH,
        )

    def share_copy(c, step):
        other = others[step]
        head, sub = c // SUBS, c % SUBS
        column = pl.multiple_of((own * heads + head) * HEAD_DIM, HEAD_DIM)
        return pltpu.make_async_remote_copy(
            src_ref=held.at[c, pl.ds(other * share, share)],
            dst_ref=fin.at[:, sub, :, pl.ds(column, HEAD_DIM)],
            send_sem=as_sem.at[c, step], recv_sem=ar_sem.at[c, step],
            device_id=(row, other), device_id_type=MESH,
        )

    chosen = [plan_ref[section, row] for section in range(SECTIONS)]
    swaps, shares = [], []

    def stage(section, c):
        if section:
            swap_copy(section - 1, c).wait_recv()
            taken = rcv[section - 1, c]
            for b in range(BLOCKS):
                lines = slice(b * GRAINS, (b + 1) * GRAINS)
                held[c, lines] = jnp.where(chosen[section - 1] == b, taken, held[c, lines])
        if section < SECTIONS:
            given = jnp.maximum(chosen[section], 0) * GRAINS
            snd[section, c] = held[c, pl.ds(given, GRAINS)]
            copy = swap_copy(section, c)
            copy.start()
            swaps.append(copy)
        else:
            for step in range(shards - 1):
                copy = share_copy(c, step)
                copy.start()
                shares.append(copy)
            head, sub = c // SUBS, c % SUBS
            column = pl.multiple_of((own * heads + head) * HEAD_DIM, HEAD_DIM)
            fin[:, sub, :, pl.ds(column, HEAD_DIM)] = held[c, pl.ds(own * share, share)]

    for step in range(chunks + SECTIONS):
        if step < chunks and step % SUBS == 0:
            attend(step // SUBS)
        if step == 0:
            pl.semaphore_wait(barrier, SECTIONS + shards - 1)
        for section in range(SECTIONS + 1):
            if 0 <= step - section < chunks:
                stage(section, step - section)

    for copy in swaps:
        copy.wait_send()
    for copy in shares:
        copy.wait()
    done = pltpu.make_async_copy(fin, out_ref, o_sem)
    done.start()
    done.wait()


def solution(mesh):
    ranks, shards = mesh.shape["dp"], mesh.shape["tensor"]
    levels = ranks.bit_length() - 1

    def local(queries, key_rows, values, doc_lengths, swap_plan):
        heads = queries.shape[1] // HEAD_DIM
        chunks = heads * SUBS
        share = BLOCKS * GRAINS // shards
        out_shape = (share, SUBS, GRAIN, shards * heads * HEAD_DIM)
        vmem = pl.BlockSpec(memory_space=pltpu.VMEM)
        smem = pl.BlockSpec(memory_space=pltpu.SMEM)

        def run(*refs):
            kernel(heads, shards, levels, *refs)

        out = pl.pallas_call(
            run,
            out_shape=jax.ShapeDtypeStruct(out_shape, jnp.bfloat16),
            in_specs=[vmem, vmem, vmem, smem, smem],
            out_specs=pl.BlockSpec(memory_space=pl.ANY),
            scratch_shapes=[
                pltpu.VMEM((chunks, BLOCKS * GRAINS, GRAIN, HEAD_DIM), jnp.bfloat16),
                pltpu.VMEM((SECTIONS, chunks, GRAINS, GRAIN, HEAD_DIM), jnp.bfloat16),
                pltpu.VMEM((SECTIONS, chunks, GRAINS, GRAIN, HEAD_DIM), jnp.bfloat16),
                pltpu.VMEM(out_shape, jnp.bfloat16),
                pltpu.SMEM((BLOCKS * TILES,), jnp.int32),
                pltpu.SemaphoreType.DMA((SECTIONS, chunks)),
                pltpu.SemaphoreType.DMA((SECTIONS, chunks)),
                pltpu.SemaphoreType.DMA((chunks, shards - 1)),
                pltpu.SemaphoreType.DMA((chunks, shards - 1)),
                pltpu.SemaphoreType.DMA,
            ],
            compiler_params=pltpu.CompilerParams(
                collective_id=0, has_side_effects=True, vmem_limit_bytes=40 * 2**20
            ),
            name="attend_swap_share",
        )(queries, key_rows, values, doc_lengths.T, swap_plan.T)
        return out.reshape(share * SUBS * GRAIN, shards * heads * HEAD_DIM)

    return jax.shard_map(
        local,
        mesh=mesh,
        in_specs=(P("dp", "tensor"), P("dp", "tensor"), P("dp", "tensor"), P(), P()),
        out_specs=P(("dp", "tensor"), None),
        check_vma=False,
    )
```

```python
import math

import jax
import jax.numpy as jnp
from jax import lax
from jax.experimental import pallas as pl
from jax.experimental.pallas import tpu as pltpu
from jax.sharding import PartitionSpec as P

HEAD_DIM = 128
SECTIONS = 4
BLOCK = 512
TILE = 128
TILES = BLOCK // TILE
BLOCKS = 3
SUBS = 4
GRAIN = 64 // SUBS
GRAINS = BLOCK // GRAIN // SUBS
LAGS = (0, 3, 5, 7, 9)
SCALE = math.log2(math.e) / math.sqrt(HEAD_DIM)
MESH = pl.DeviceIdType.MESH


def kernel(
    heads, shards, levels,
    q_hbm, k_hbm, v_hbm, len_hbm, plan_hbm, out_ref,
    q_ref, k_ref, v_ref, len_ref, plan_ref, ids, held, snd, rcv,
    in_sem, s_sem, r_sem, as_sem, ar_sem, o_sem,
):
    row = lax.axis_index("dp")
    own = lax.axis_index("tensor")
    chunks = heads * SUBS
    share = BLOCKS * GRAINS // shards

    partners = []
    for section in range(SECTIONS):
        mask = 2 ** (levels - 1 - section)
        partners.append(row + mask * (1 - 2 * ((row // mask) % 2)))
    others = [(own + step) % shards for step in range(1, shards)]

    barrier = pltpu.get_barrier_semaphore()
    for partner in partners:
        pl.semaphore_signal(barrier, inc=1, device_id=(partner, own), device_id_type=MESH)
    for other in others:
        pl.semaphore_signal(barrier, inc=1, device_id=(row, other), device_id_type=MESH)

    def query_copy(head):
        columns = pl.ds(pl.multiple_of(head * HEAD_DIM, HEAD_DIM), HEAD_DIM)
        return pltpu.make_async_copy(q_hbm.at[:, columns], q_ref.at[head], in_sem.at[head])

    fetches = [
        pltpu.make_async_copy(source, target, in_sem.at[heads + at])
        for at, (source, target) in enumerate(
            [(len_hbm, len_ref), (plan_hbm, plan_ref), (k_hbm, k_ref), (v_hbm, v_ref)]
        )
    ]
    for fetch in fetches[:3] + [query_copy(0)] + fetches[3:]:
        fetch.start()
    for head in range(1, heads):
        query_copy(head).start()

    fetches[0].wait()
    endings = []
    total = jnp.int32(0)
    for doc in range(len_ref.shape[0]):
        total = total + len_ref[doc, row]
        endings.append(total)
    for tile in range(BLOCKS * TILES):
        count = jnp.int32(0)
        for ending in endings:
            count = count + jnp.where(ending <= tile * TILE, 1, 0)
        ids[tile] = jnp.where(tile * TILE < total, count, -1)
    for fetch in fetches[1:]:
        fetch.wait()

    lower = lax.broadcasted_iota(jnp.int32, (TILE, TILE), 0) >= lax.broadcasted_iota(
        jnp.int32, (TILE, TILE), 1
    )

    def attend(head):
        query_copy(head).wait()

        def block(b, carry):
            start = pl.multiple_of(b * BLOCK, BLOCK)
            for i in range(TILES):
                keys = k_ref[pl.ds(start, (i + 1) * TILE), :]
                scores = lax.dot_general(
                    q_ref[head, pl.ds(start + i * TILE, TILE), :], keys,
                    (((1,), (1,)), ((), ())), preferred_element_type=jnp.float32,
                )
                doc = ids[b * TILES + i]
                parts = [
                    scores[:, j * TILE : (j + 1) * TILE]
                    + jnp.where(ids[b * TILES + j] == doc, 0.0, -1e30)
                    for j in range(i)
                ]
                parts.append(jnp.where(lower, scores[:, i * TILE :], -1e30))
                masked = jnp.concatenate(parts, axis=1) if i else parts[0]
                highest = jnp.max(masked, axis=1, keepdims=True)
                powers = jnp.exp2((masked - highest) * SCALE)
                live = jnp.where(doc >= 0, 1.0, 0.0)
                weights = powers * (live / jnp.sum(powers, axis=1, keepdims=True))
                mixed = jnp.dot(
                    weights.astype(jnp.bfloat16), v_ref[pl.ds(start, (i + 1) * TILE), :],
                    preferred_element_type=jnp.float32,
                ).astype(jnp.bfloat16)
                for g in range(TILE // GRAIN):
                    at = i * (TILE // GRAIN) + g
                    held[head * SUBS + at % SUBS, b * GRAINS + at // SUBS] = mixed[
                        g * GRAIN : (g + 1) * GRAIN
                    ]
            return carry

        lax.fori_loop(0, BLOCKS, block, 0)

    def swap_copy(section, c):
        return pltpu.make_async_remote_copy(
            src_ref=snd.at[section, c], dst_ref=rcv.at[section, c],
            send_sem=s_sem.at[section], recv_sem=r_sem.at[section, c],
            device_id=(partners[section], own), device_id_type=MESH,
        )

    def share_copy(c, other):
        head, sub = c // SUBS, c % SUBS
        columns = pl.ds(pl.multiple_of((own * heads + head) * HEAD_DIM, HEAD_DIM), HEAD_DIM)
        return pltpu.make_async_remote_copy(
            src_ref=held.at[c, pl.ds(other * share, share)],
            dst_ref=out_ref.at[:, sub, :, columns],
            send_sem=as_sem, recv_sem=ar_sem,
            device_id=(row, other), device_id_type=MESH,
        )

    def stage(section, c):
        if section:
            swap_copy(section - 1, c).wait_recv()
            taken = rcv[section - 1, c]
            chosen = plan_ref[section - 1, row]
            for b in range(BLOCKS):
                lines = slice(b * GRAINS, (b + 1) * GRAINS)
                held[c, lines] = jnp.where(chosen == b, taken, held[c, lines])
        if section < SECTIONS:
            given = jnp.maximum(plan_ref[section, row], 0) * GRAINS
            snd[section, c] = held[c, pl.ds(given, GRAINS)]
            swap_copy(section, c).start()
        else:
            for other in others:
                share_copy(c, other).start()
            head, sub = c // SUBS, c % SUBS
            columns = pl.ds(pl.multiple_of((own * heads + head) * HEAD_DIM, HEAD_DIM), HEAD_DIM)
            pltpu.make_async_copy(held.at[c, pl.ds(own * share, share)], out_ref.at[:, sub, :, columns], o_sem).start()

    attend(0)
    pl.semaphore_wait(barrier, SECTIONS + shards - 1)

    def step(k, carry):
        @pl.when((k > 0) & (k < chunks) & (k % SUBS == 0))
        def _():
            attend(k // SUBS)

        for section in reversed(range(SECTIONS + 1)):
            c = k - LAGS[section]

            @pl.when((c >= 0) & (c < chunks))
            def _(section=section, c=c):
                stage(section, c)

        return carry

    lax.fori_loop(0, chunks + LAGS[-1], step, 0)

    for section in range(SECTIONS):
        pltpu.make_async_copy(snd.at[section], rcv.at[section], s_sem.at[section]).wait()
    moved = out_ref.at[:, :, :, pl.ds(0, (shards - 1) * heads * HEAD_DIM)]
    pltpu.make_async_copy(moved, moved, as_sem).wait()
    pltpu.make_async_copy(moved, moved, ar_sem).wait()
    kept = out_ref.at[:, :, :, pl.ds(0, heads * HEAD_DIM)]
    pltpu.make_async_copy(kept, kept, o_sem).wait()


def solution(mesh):
    ranks, shards = mesh.shape["dp"], mesh.shape["tensor"]
    levels = ranks.bit_length() - 1

    def local(queries, key_rows, values, doc_lengths, swap_plan):
        tokens, heads = queries.shape[0], queries.shape[1] // HEAD_DIM
        chunks = heads * SUBS
        share = BLOCKS * GRAINS // shards
        out_shape = (share, SUBS, GRAIN, shards * heads * HEAD_DIM)
        lengths, plan = doc_lengths.T, swap_plan.T

        def run(*refs):
            kernel(heads, shards, levels, *refs)

        out = pl.pallas_call(
            run,
            out_shape=pltpu.VMEM(out_shape, jnp.bfloat16),
            in_specs=[pl.BlockSpec(memory_space=pltpu.HBM)] * 5,
            out_specs=pl.BlockSpec(memory_space=pltpu.VMEM),
            scratch_shapes=[
                pltpu.VMEM((heads, tokens, HEAD_DIM), jnp.bfloat16),
                pltpu.VMEM((tokens, HEAD_DIM), jnp.bfloat16),
                pltpu.VMEM((tokens, HEAD_DIM), jnp.bfloat16),
                pltpu.SMEM(lengths.shape, jnp.int32),
                pltpu.SMEM(plan.shape, jnp.int32),
                pltpu.SMEM((BLOCKS * TILES,), jnp.int32),
                pltpu.VMEM((chunks, BLOCKS * GRAINS, GRAIN, HEAD_DIM), jnp.bfloat16),
                pltpu.VMEM((SECTIONS, chunks, GRAINS, GRAIN, HEAD_DIM), jnp.bfloat16),
                pltpu.VMEM((SECTIONS, chunks, GRAINS, GRAIN, HEAD_DIM), jnp.bfloat16),
                pltpu.SemaphoreType.DMA((heads + 4,)),
                pltpu.SemaphoreType.DMA((SECTIONS,)),
                pltpu.SemaphoreType.DMA((SECTIONS, chunks)),
                pltpu.SemaphoreType.DMA,
                pltpu.SemaphoreType.DMA,
                pltpu.SemaphoreType.DMA,
            ],
            compiler_params=pltpu.CompilerParams(
                collective_id=0, has_side_effects=True, vmem_limit_bytes=56 * 2**20
            ),
            name="attend_swap_share",
        )(queries, key_rows, values, lengths, plan)
        return out.reshape(share * SUBS * GRAIN, shards * heads * HEAD_DIM)

    return jax.shard_map(
        local,
        mesh=mesh,
        in_specs=(P("dp", "tensor"), P("dp", "tensor"), P("dp", "tensor"), P(), P()),
        out_specs=P(("dp", "tensor"), None),
        check_vma=False,
    )
```

```python
import math

import jax
import jax.numpy as jnp
from jax import lax
from jax.experimental import pallas as pl
from jax.experimental.pallas import tpu as pltpu
from jax.sharding import PartitionSpec as P

HEAD_DIM = 128
SECTIONS = 4
BLOCK = 512
TILE = 128
TILES = BLOCK // TILE
BLOCKS = 3
SUBS = 4
GRAIN = 64 // SUBS
GRAINS = BLOCK // GRAIN // SUBS
LAGS = ((0, 5, 8, 10, 12), (0, 3, 5, 7, 9))
SCALE = math.log2(math.e) / math.sqrt(HEAD_DIM)
MESH = pl.DeviceIdType.MESH


def kernel(
    heads, shards, levels,
    q_hbm, k_hbm, v_hbm, len_hbm, plan_hbm, out_ref,
    q_ref, k_ref, v_ref, len_ref, plan_ref, ids, held, snd, rcv,
    in_sem, s_sem, r_sem, as_sem, ar_sem, o_sem,
):
    row = lax.axis_index("dp")
    own = lax.axis_index("tensor")
    chunks = heads * SUBS
    share = BLOCKS * GRAINS // shards

    partners = []
    for section in range(SECTIONS):
        mask = 2 ** (levels - 1 - section)
        partners.append(row + mask * (1 - 2 * ((row // mask) % 2)))
    others = [(own + step) % shards for step in range(1, shards)]

    barrier = pltpu.get_barrier_semaphore()
    for partner in partners:
        pl.semaphore_signal(barrier, inc=1, device_id=(partner, own), device_id_type=MESH)
    for other in others:
        pl.semaphore_signal(barrier, inc=1, device_id=(row, other), device_id_type=MESH)

    def query_copy(head):
        columns = pl.ds(pl.multiple_of(head * HEAD_DIM, HEAD_DIM), HEAD_DIM)
        return pltpu.make_async_copy(q_hbm.at[:, columns], q_ref.at[head], in_sem.at[head])

    fetches = [
        pltpu.make_async_copy(source, target, in_sem.at[heads + at])
        for at, (source, target) in enumerate(
            [(len_hbm, len_ref), (plan_hbm, plan_ref), (k_hbm, k_ref), (v_hbm, v_ref)]
        )
    ]
    for fetch in fetches[:3] + [query_copy(0)] + fetches[3:]:
        fetch.start()
    for head in range(1, heads):
        query_copy(head).start()

    fetches[0].wait()
    endings = []
    total = jnp.int32(0)
    for doc in range(len_ref.shape[0]):
        total = total + len_ref[doc, row]
        endings.append(total)
    for tile in range(BLOCKS * TILES):
        count = jnp.int32(0)
        for ending in endings:
            count = count + jnp.where(ending <= tile * TILE, 1, 0)
        ids[tile] = jnp.where(tile * TILE < total, count, -1)
    for fetch in fetches[1:]:
        fetch.wait()

    lower = lax.broadcasted_iota(jnp.int32, (TILE, TILE), 0) >= lax.broadcasted_iota(
        jnp.int32, (TILE, TILE), 1
    )

    def attend(head):
        query_copy(head).wait()

        def block(b, carry):
            start = pl.multiple_of(b * BLOCK, BLOCK)
            for i in range(TILES):
                keys = k_ref[pl.ds(start, (i + 1) * TILE), :]
                scores = lax.dot_general(
                    q_ref[head, pl.ds(start + i * TILE, TILE), :], keys,
                    (((1,), (1,)), ((), ())), preferred_element_type=jnp.float32,
                )
                doc = ids[b * TILES + i]
                parts = [
                    scores[:, j * TILE : (j + 1) * TILE]
                    + jnp.where(ids[b * TILES + j] == doc, 0.0, -1e30)
                    for j in range(i)
                ]
                parts.append(jnp.where(lower, scores[:, i * TILE :], -1e30))
                masked = jnp.concatenate(parts, axis=1) if i else parts[0]
                highest = jnp.max(masked, axis=1, keepdims=True)
                powers = jnp.exp2((masked - highest) * SCALE)
                live = jnp.where(doc >= 0, 1.0, 0.0)
                weights = powers * (live / jnp.sum(powers, axis=1, keepdims=True))
                mixed = jnp.dot(
                    weights.astype(jnp.bfloat16), v_ref[pl.ds(start, (i + 1) * TILE), :],
                    preferred_element_type=jnp.float32,
                ).astype(jnp.bfloat16)
                for g in range(TILE // GRAIN):
                    at = i * (TILE // GRAIN) + g
                    held[head * SUBS + at % SUBS, b * GRAINS + at // SUBS] = mixed[
                        g * GRAIN : (g + 1) * GRAIN
                    ]
            return carry

        lax.fori_loop(0, BLOCKS, block, 0)

    def swap_copy(section, c):
        return pltpu.make_async_remote_copy(
            src_ref=snd.at[section, c], dst_ref=rcv.at[section, c],
            send_sem=s_sem.at[section], recv_sem=r_sem.at[section, c],
            device_id=(partners[section], own), device_id_type=MESH,
        )

    def share_copy(c, other):
        head, sub = c // SUBS, c % SUBS
        columns = pl.ds(pl.multiple_of((own * heads + head) * HEAD_DIM, HEAD_DIM), HEAD_DIM)
        return pltpu.make_async_remote_copy(
            src_ref=held.at[c, pl.ds(other * share, share)],
            dst_ref=out_ref.at[:, sub, :, columns],
            send_sem=as_sem, recv_sem=ar_sem,
            device_id=(row, other), device_id_type=MESH,
        )

    def stage(section, c):
        if section:
            swap_copy(section - 1, c).wait_recv()
            taken = rcv[section - 1, c]
            chosen = plan_ref[section - 1, row]
            for b in range(BLOCKS):
                lines = slice(b * GRAINS, (b + 1) * GRAINS)
                held[c, lines] = jnp.where(chosen == b, taken, held[c, lines])
        if section < SECTIONS:
            given = jnp.maximum(plan_ref[section, row], 0) * GRAINS
            snd[section, c] = held[c, pl.ds(given, GRAINS)]
            swap_copy(section, c).start()
        else:
            for other in others:
                share_copy(c, other).start()
            head, sub = c // SUBS, c % SUBS
            columns = pl.ds(pl.multiple_of((own * heads + head) * HEAD_DIM, HEAD_DIM), HEAD_DIM)
            pltpu.make_async_copy(held.at[c, pl.ds(own * share, share)], out_ref.at[:, sub, :, columns], o_sem).start()

    lags = [even + (odd - even) * (row % 2) for even, odd in zip(*LAGS)]
    attend(0)
    pl.semaphore_wait(barrier, SECTIONS + shards - 1)

    def step(k, carry):
        @pl.when((k > 0) & (k < chunks) & (k % SUBS == 0))
        def _():
            attend(k // SUBS)

        for section in reversed(range(SECTIONS + 1)):
            c = k - lags[section]

            @pl.when((c >= 0) & (c < chunks))
            def _(section=section, c=c):
                stage(section, c)

        return carry

    lax.fori_loop(0, chunks + lags[-1], step, 0)

    for section in range(SECTIONS):
        pltpu.make_async_copy(snd.at[section], rcv.at[section], s_sem.at[section]).wait()
    moved = out_ref.at[:, :, :, pl.ds(0, (shards - 1) * heads * HEAD_DIM)]
    pltpu.make_async_copy(moved, moved, as_sem).wait()
    pltpu.make_async_copy(moved, moved, ar_sem).wait()
    kept = out_ref.at[:, :, :, pl.ds(0, heads * HEAD_DIM)]
    pltpu.make_async_copy(kept, kept, o_sem).wait()


def solution(mesh):
    ranks, shards = mesh.shape["dp"], mesh.shape["tensor"]
    levels = ranks.bit_length() - 1

    def local(queries, key_rows, values, doc_lengths, swap_plan):
        tokens, heads = queries.shape[0], queries.shape[1] // HEAD_DIM
        chunks = heads * SUBS
        share = BLOCKS * GRAINS // shards
        out_shape = (share, SUBS, GRAIN, shards * heads * HEAD_DIM)
        lengths, plan = doc_lengths.T, swap_plan.T

        def run(*refs):
            kernel(heads, shards, levels, *refs)

        out = pl.pallas_call(
            run,
            out_shape=pltpu.VMEM(out_shape, jnp.bfloat16),
            in_specs=[pl.BlockSpec(memory_space=pltpu.HBM)] * 5,
            out_specs=pl.BlockSpec(memory_space=pltpu.VMEM),
            scratch_shapes=[
                pltpu.VMEM((heads, tokens, HEAD_DIM), jnp.bfloat16),
                pltpu.VMEM((tokens, HEAD_DIM), jnp.bfloat16),
                pltpu.VMEM((tokens, HEAD_DIM), jnp.bfloat16),
                pltpu.SMEM(lengths.shape, jnp.int32),
                pltpu.SMEM(plan.shape, jnp.int32),
                pltpu.SMEM((BLOCKS * TILES,), jnp.int32),
                pltpu.VMEM((chunks, BLOCKS * GRAINS, GRAIN, HEAD_DIM), jnp.bfloat16),
                pltpu.VMEM((SECTIONS, chunks, GRAINS, GRAIN, HEAD_DIM), jnp.bfloat16),
                pltpu.VMEM((SECTIONS, chunks, GRAINS, GRAIN, HEAD_DIM), jnp.bfloat16),
                pltpu.SemaphoreType.DMA((heads + 4,)),
                pltpu.SemaphoreType.DMA((SECTIONS,)),
                pltpu.SemaphoreType.DMA((SECTIONS, chunks)),
                pltpu.SemaphoreType.DMA,
                pltpu.SemaphoreType.DMA,
                pltpu.SemaphoreType.DMA,
            ],
            compiler_params=pltpu.CompilerParams(
                collective_id=0, has_side_effects=True, vmem_limit_bytes=56 * 2**20
            ),
            name="attend_swap_share",
        )(queries, key_rows, values, lengths, plan)
        return out.reshape(share * SUBS * GRAIN, shards * heads * HEAD_DIM)

    return jax.shard_map(
        local,
        mesh=mesh,
        in_specs=(P("dp", "tensor"), P("dp", "tensor"), P("dp", "tensor"), P(), P()),
        out_specs=P(("dp", "tensor"), None),
        check_vma=False,
    )
```

```python
import math

import jax
import jax.numpy as jnp
from jax import lax
from jax.experimental import pallas as pl
from jax.experimental.pallas import tpu as pltpu
from jax.sharding import PartitionSpec as P

HEAD_DIM = 128
SECTIONS = 4
BLOCK = 512
TILE = 128
TILES = BLOCK // TILE
BLOCKS = 3
SUBS = 4
GRAIN = 64 // SUBS
GRAINS = BLOCK // GRAIN // SUBS
LAGS = ((0, 5, 8, 10, 12), (0, 3, 5, 7, 9))
SCALE = math.log2(math.e) / math.sqrt(HEAD_DIM)
MESH = pl.DeviceIdType.MESH


def kernel(
    heads, shards, levels,
    q_hbm, k_hbm, v_hbm, len_hbm, plan_hbm, out_ref,
    q_ref, k_ref, v_ref, len_ref, plan_ref, ids, held, snd, rcv,
    in_sem, s_sem, r_sem, as_sem, ar_sem, o_sem,
):
    row = lax.axis_index("dp")
    own = lax.axis_index("tensor")
    chunks = heads * SUBS
    share = BLOCKS * GRAINS // shards

    partners = []
    for section in range(SECTIONS):
        mask = 2 ** (levels - 1 - section)
        partners.append(row + mask * (1 - 2 * ((row // mask) % 2)))
    others = [(own + step) % shards for step in range(1, shards)]
    swap_numbers = [partner * shards + own for partner in partners]
    far_first = sorted(range(1, shards), key=lambda step: -min(step, shards - step))

    barrier = pltpu.get_barrier_semaphore()
    for partner in partners:
        pl.semaphore_signal(barrier, inc=1, device_id=(partner, own), device_id_type=MESH)
    for step in far_first:
        other = (own + step) % shards
        pl.semaphore_signal(barrier, inc=1, device_id=(row, other), device_id_type=MESH)

    def query_copy(head):
        columns = pl.ds(pl.multiple_of(head * HEAD_DIM, HEAD_DIM), HEAD_DIM)
        return pltpu.make_async_copy(q_hbm.at[:, columns], q_ref.at[head], in_sem.at[head])

    fetches = [
        pltpu.make_async_copy(source, target, in_sem.at[heads + at])
        for at, (source, target) in enumerate(
            [(len_hbm, len_ref), (plan_hbm, plan_ref), (k_hbm, k_ref), (v_hbm, v_ref)]
        )
    ]
    for fetch in fetches[:3] + [query_copy(0)] + fetches[3:]:
        fetch.start()
    for head in range(1, heads):
        query_copy(head).start()

    fetches[0].wait()
    endings = []
    total = jnp.int32(0)
    for doc in range(len_ref.shape[0]):
        total = total + len_ref[doc, row]
        endings.append(total)
    for tile in range(BLOCKS * TILES):
        count = jnp.int32(0)
        for ending in endings:
            count = count + jnp.where(ending <= tile * TILE, 1, 0)
        ids[tile] = jnp.where(tile * TILE < total, count, -1)
    for fetch in fetches[1:]:
        fetch.wait()

    lower = lax.broadcasted_iota(jnp.int32, (TILE, TILE), 0) >= lax.broadcasted_iota(
        jnp.int32, (TILE, TILE), 1
    )

    def attend(head):
        query_copy(head).wait()

        def block(b, carry):
            start = pl.multiple_of(b * BLOCK, BLOCK)
            for i in range(TILES):
                keys = k_ref[pl.ds(start, (i + 1) * TILE), :]
                scores = lax.dot_general(
                    q_ref[head, pl.ds(start + i * TILE, TILE), :], keys,
                    (((1,), (1,)), ((), ())), preferred_element_type=jnp.float32,
                )
                doc = ids[b * TILES + i]
                parts = [
                    scores[:, j * TILE : (j + 1) * TILE]
                    + jnp.where(ids[b * TILES + j] == doc, 0.0, -1e30)
                    for j in range(i)
                ]
                parts.append(jnp.where(lower, scores[:, i * TILE :], -1e30))
                masked = jnp.concatenate(parts, axis=1) if i else parts[0]
                highest = jnp.max(masked, axis=1, keepdims=True)
                powers = jnp.exp2((masked - highest) * SCALE)
                live = jnp.where(doc >= 0, 1.0, 0.0)
                weights = powers * (live / jnp.sum(powers, axis=1, keepdims=True))
                mixed = jnp.dot(
                    weights.astype(jnp.bfloat16), v_ref[pl.ds(start, (i + 1) * TILE), :],
                    preferred_element_type=jnp.float32,
                ).astype(jnp.bfloat16)
                for g in range(TILE // GRAIN):
                    at = i * (TILE // GRAIN) + g
                    held[head * SUBS + at % SUBS, b * GRAINS + at // SUBS] = mixed[
                        g * GRAIN : (g + 1) * GRAIN
                    ]
            return carry

        lax.fori_loop(0, BLOCKS, block, 0)

    def swap_copy(section, c):
        return pltpu.make_async_remote_copy(
            src_ref=snd.at[section, c], dst_ref=rcv.at[section, c],
            send_sem=s_sem.at[section], recv_sem=r_sem.at[section, c],
            device_id=swap_numbers[section], device_id_type=pl.DeviceIdType.LOGICAL,
        )

    def share_copy(c, other):
        head, sub = c // SUBS, c % SUBS
        columns = pl.ds(pl.multiple_of((own * heads + head) * HEAD_DIM, HEAD_DIM), HEAD_DIM)
        return pltpu.make_async_remote_copy(
            src_ref=held.at[c, pl.ds(other * share, share)],
            dst_ref=out_ref.at[:, sub, :, columns],
            send_sem=as_sem, recv_sem=ar_sem,
            device_id=row * shards + other, device_id_type=pl.DeviceIdType.LOGICAL,
        )

    def stage(section, c):
        if section:
            swap_copy(section - 1, c).wait_recv()
            taken = rcv[section - 1, c]
            chosen = plan_ref[section - 1, row]
            for b in range(BLOCKS):
                lines = slice(b * GRAINS, (b + 1) * GRAINS)
                held[c, lines] = jnp.where(chosen == b, taken, held[c, lines])
        if section < SECTIONS:
            given = jnp.maximum(plan_ref[section, row], 0) * GRAINS
            snd[section, c] = held[c, pl.ds(given, GRAINS)]
            swap_copy(section, c).start()
        else:
            for other in others:
                share_copy(c, other).start()
            head, sub = c // SUBS, c % SUBS
            columns = pl.ds(pl.multiple_of((own * heads + head) * HEAD_DIM, HEAD_DIM), HEAD_DIM)
            pltpu.make_async_copy(held.at[c, pl.ds(own * share, share)], out_ref.at[:, sub, :, columns], o_sem).start()

    lags = [even + (odd - even) * (row % 2) for even, odd in zip(*LAGS)]
    attend(0)
    pl.semaphore_wait(barrier, SECTIONS + shards - 1)

    def step(k, carry):
        @pl.when((k > 0) & (k < chunks) & (k % SUBS == 0))
        def _():
            attend(k // SUBS)

        for section in reversed(range(SECTIONS + 1)):
            c = k - lags[section]

            @pl.when((c >= 0) & (c < chunks))
            def _(section=section, c=c):
                stage(section, c)

        return carry

    lax.fori_loop(0, chunks + lags[-1], step, 0)

    for section in range(SECTIONS):
        pltpu.make_async_copy(snd.at[section], rcv.at[section], s_sem.at[section]).wait()
    moved = out_ref.at[:, :, :, pl.ds(0, (shards - 1) * heads * HEAD_DIM)]
    pltpu.make_async_copy(moved, moved, as_sem).wait()
    pltpu.make_async_copy(moved, moved, ar_sem).wait()
    kept = out_ref.at[:, :, :, pl.ds(0, heads * HEAD_DIM)]
    pltpu.make_async_copy(kept, kept, o_sem).wait()


def solution(mesh):
    ranks, shards = mesh.shape["dp"], mesh.shape["tensor"]
    levels = ranks.bit_length() - 1

    def local(queries, key_rows, values, doc_lengths, swap_plan):
        tokens, heads = queries.shape[0], queries.shape[1] // HEAD_DIM
        chunks = heads * SUBS
        share = BLOCKS * GRAINS // shards
        out_shape = (share, SUBS, GRAIN, shards * heads * HEAD_DIM)
        lengths, plan = doc_lengths.T, swap_plan.T

        def run(*refs):
            kernel(heads, shards, levels, *refs)

        out = pl.pallas_call(
            run,
            out_shape=pltpu.VMEM(out_shape, jnp.bfloat16),
            in_specs=[pl.BlockSpec(memory_space=pltpu.HBM)] * 5,
            out_specs=pl.BlockSpec(memory_space=pltpu.VMEM),
            scratch_shapes=[
                pltpu.VMEM((heads, tokens, HEAD_DIM), jnp.bfloat16),
                pltpu.VMEM((tokens, HEAD_DIM), jnp.bfloat16),
                pltpu.VMEM((tokens, HEAD_DIM), jnp.bfloat16),
                pltpu.SMEM(lengths.shape, jnp.int32),
                pltpu.SMEM(plan.shape, jnp.int32),
                pltpu.SMEM((BLOCKS * TILES,), jnp.int32),
                pltpu.VMEM((chunks, BLOCKS * GRAINS, GRAIN, HEAD_DIM), jnp.bfloat16),
                pltpu.VMEM((SECTIONS, chunks, GRAINS, GRAIN, HEAD_DIM), jnp.bfloat16),
                pltpu.VMEM((SECTIONS, chunks, GRAINS, GRAIN, HEAD_DIM), jnp.bfloat16),
                pltpu.SemaphoreType.DMA((heads + 4,)),
                pltpu.SemaphoreType.DMA((SECTIONS,)),
                pltpu.SemaphoreType.DMA((SECTIONS, chunks)),
                pltpu.SemaphoreType.DMA,
                pltpu.SemaphoreType.DMA,
                pltpu.SemaphoreType.DMA,
            ],
            compiler_params=pltpu.CompilerParams(
                collective_id=0, has_side_effects=True, vmem_limit_bytes=56 * 2**20
            ),
            name="attend_swap_share",
        )(queries, key_rows, values, lengths, plan)
        return out.reshape(share * SUBS * GRAIN, shards * heads * HEAD_DIM)

    return jax.shard_map(
        local,
        mesh=mesh,
        in_specs=(P("dp", "tensor"), P("dp", "tensor"), P("dp", "tensor"), P(), P()),
        out_specs=P(("dp", "tensor"), None),
        check_vma=False,
    )
```
